32 devices in a mesh: ga: 4 (over z), orb: 8 (over y, x, core).
Axes of the slice: x: 2, y: 2, z: 4, core: 2. Of those that a mesh axis runs over, the one named last changes fastest.
Arguments:
- coefficients: bfloat16 [2, 294912, 512], P(None, ('ga', 'orb')), may hold values from -0.01171875 to 0.01171875
- triples: int32 [3, 294912], P(None, ('ga', 'orb')), may hold values from -33 to 33
- elec_pos: float32 [3, 32], P(None, ('ga', 'orb')), may hold values from 0 to 1
- ion_pos: float32 [3, 128], replicated, may hold values from 0 to 1
- assignment: int32 [32], P(('ga', 'orb')), may hold values from 0 to 127
- rotation: int32 [32], P(('ga', 'orb')), may hold values from 0 to 63
- quad_table: float32 [64, 3, 12], replicated, may hold values from -2.4 to 2.4
- inverse_rows: float32 [32, 512], P(('ga', 'orb')), may hold values from -0.25 to 0.25
Outputs:
- ratios: float32 [32, 12], P(('ga', 'orb'))
The draws below stay inside these ranges and needn't reach their ends.
All inputs are finite; a program needn't handle non-finite values.
Results may differ from the reference program's by a relative error of at most 0.0024.
Values may be sent and summed in bfloat16 or wider, within the bound.
A program may use at most 64 MiB of HBM per device.

```python
import math
import jax
import jax.numpy as jnp
from jax import lax

NORB = 512
NG = 294912
Q = 12
NION = 128
NROT = 64
NEV = 32


def touch_ends(array, rng, low, high):
    dims = array.shape
    spot = [jax.random.randint(jax.random.fold_in(rng, axis), (), 0, dims[axis]) for axis in range(len(dims))]
    array = array.at[tuple(spot)].set(low)
    longest = dims.index(max(dims))
    spot[longest] = (spot[longest] + 1) % dims[longest]
    return array.at[tuple(spot)].set(high)


def levels(key, shape, cuts, least, largest):
    gain = 1.0
    for dim, blocks in cuts:
        draws = jax.random.uniform(jax.random.fold_in(jax.random.fold_in(key, 6), dim), (blocks,), jnp.float32, least / len(cuts), largest / len(cuts))
        gain = gain * jnp.repeat(jnp.exp(draws), shape[dim] // blocks).reshape((-1,) + (1,) * (len(shape) - 1 - dim))
    return gain


def centred(rng, extent, spread, bound, split=(), held_as=jnp.bfloat16):
    level = levels(rng, extent, split, -0.22, 0.18) if split else 1.0
    result = jax.random.normal(rng, extent, jnp.float32) * spread * level
    return jnp.minimum(jnp.maximum(result, -bound), bound).astype(held_as)


def setup_inputs(seed: int = 0) -> dict:
    key_of = jax.random.split(jax.random.key(seed), 9)
    coefficients = centred(key_of[0], (2, NG, NORB), NG ** -0.5, 0.01171875, ((1, 32),))
    triples = touch_ends(jax.random.randint(key_of[1], (3, NG), -33, 34), jax.random.fold_in(key_of[1], 1), -33, 33).astype(jnp.int32)
    elec_pos = jnp.clip(1.0 * jax.random.uniform(key_of[2], (3, NEV), jnp.float32) ** levels(key_of[2], (3, NEV), ((1, 32),), -0.2, 0.2), 0.0, 1.0)
    ion_pos = jnp.clip(jax.random.uniform(key_of[3], (3, NION), jnp.float32, 0.0, 1.0), 0.0, 1.0)
    assignment = touch_ends(jax.random.randint(key_of[4], (NEV,), 0, NION), jax.random.fold_in(key_of[4], 1), 0, NION - 1).astype(jnp.int32)
    rotation = touch_ends(jax.random.randint(key_of[5], (NEV,), 0, NROT), jax.random.fold_in(key_of[5], 1), 0, NROT - 1).astype(jnp.int32)
    quad_table = centred(key_of[6], (NROT, 3, Q), 0.4, 2.4, (), jnp.float32)
    inverse_rows = centred(key_of[7], (NEV, NORB), NORB ** -0.5, 0.25, ((0, 32),), jnp.float32)
    return dict(coefficients=coefficients, triples=triples, elec_pos=elec_pos, ion_pos=ion_pos, assignment=assignment, rotation=rotation, quad_table=quad_table, inverse_rows=inverse_rows)


TWO_PI = 2.0 * math.pi

def point_coords(elec_pos, ion_pos, assignment, rotation, quad_table):
    ion_rows = jnp.take(ion_pos, assignment, axis=1)
    offsets = elec_pos - ion_rows
    radius = jnp.sqrt(lax.optimization_barrier(jnp.sum(offsets * offsets, axis=0)))
    displace = jnp.take(quad_table, rotation, axis=0)
    located = ion_rows.T[:, :, None] + radius[:, None, None] * displace
    return jnp.transpose(located, (1, 0, 2)).reshape(3, -1)

def phase_values(points, triples, coefficients):
    point_count = points.shape[1]
    wave_count = triples.shape[1]
    columns = coefficients.shape[2]
    block_rows = math.gcd(point_count, 512)
    span_cols = wave_count if wave_count <= 4096 else math.gcd(wave_count, 4096)
    waves = triples.astype(jnp.float32) * TWO_PI

    def one_block(block_points):

        def add_panel(step_index, running):
            offset = step_index * span_cols
            wave_part = lax.dynamic_slice_in_dim(waves, offset, span_cols, 1)
            angle = block_points[0][:, None] * wave_part[0][None, :] + block_points[1][:, None] * wave_part[1][None, :] + block_points[2][:, None] * wave_part[2][None, :]
            phases = jnp.concatenate([jnp.cos(angle).astype(jnp.bfloat16), jnp.sin(angle).astype(jnp.bfloat16)], axis=1)
            weights = lax.dynamic_slice_in_dim(coefficients, offset, span_cols, 1).reshape(2 * span_cols, columns)
            return running + jnp.dot(phases, weights, preferred_element_type=jnp.float32)
        initial = jnp.zeros((block_rows, columns), jnp.float32)
        return lax.fori_loop(0, wave_count // span_cols, add_panel, initial)
    blocks = jnp.transpose(points.reshape(3, point_count // block_rows, block_rows), (1, 0, 2))
    return lax.map(one_block, blocks).reshape(point_count, columns)

def reference(coefficients, triples, elec_pos, ion_pos, assignment, rotation, quad_table, inverse_rows):
    points = point_coords(elec_pos, ion_pos, assignment, rotation, quad_table)
    values = phase_values(points, triples, coefficients)
    electrons = inverse_rows.shape[0]
    shaped = values.reshape(electrons, values.shape[0] // electrons, values.shape[1])
    return lax.optimization_barrier(jnp.sum(shaped * inverse_rows[:, None, :], axis=2))
```

```python
import functools
import math

import jax
import jax.numpy as jnp
from jax import lax
from jax.experimental import pallas as pl
from jax.experimental.pallas import tpu as pltpu
from jax.sharding import PartitionSpec as P

MESH = pl.DeviceIdType.MESH
LANES = 128
SIN = (4.4409175764498094, -7.256811405668293, 3.2296557608294836)
COS = (1.4141797907346831, -6.976861782062955, 5.7090010941235345, -1.7141125404832036)
LAST = (((1,), (1,)), ((), ()))


def in_three(x):
    high = x.astype(jnp.bfloat16).astype(jnp.float32)
    rest = x - high
    middle = rest.astype(jnp.bfloat16).astype(jnp.float32)
    return high, middle, (rest - middle).astype(jnp.bfloat16).astype(jnp.float32)


def kernel(
    n_ga, n_orb, quad_count,
    coef, triples, elec, ions, assign, rot, quad, inv, out,
    held, held_sem, gathered, waves, spread, rows, phase_lhs, weight, angle, acc, total,
    outgoing, incoming, send_a, recv_a, send_b, recv_b,
):
    count = n_ga * n_orb
    me = lax.axis_index("ga") * n_orb + lax.axis_index("orb")
    chunks, _, span, columns = held.shape

    def coef_copy(c):
        return pltpu.make_async_copy(
            coef.at[:, pl.ds(c * span, span), :], held.at[c], held_sem.at[c]
        )

    def peer(i):
        other = lax.rem(me + i, count)
        return other, (other // n_orb, lax.rem(other, n_orb))

    barrier = pltpu.get_barrier_semaphore()

    def greet(i, carry):
        pl.semaphore_signal(barrier, inc=1, device_id=peer(i)[1], device_id_type=MESH)
        return carry

    lax.fori_loop(1, count, greet, 0)
    for c in range(chunks):
        coef_copy(c).start()

    lane = lax.broadcasted_iota(jnp.int32, ions.shape, 1)
    ion_row = jnp.sum(jnp.where(lane == assign[0], ions[...], 0.0), axis=1, keepdims=True)
    offset = elec[...] - ion_row
    radius = jnp.sqrt(jnp.sum(offset * offset, axis=0, keepdims=True))
    points = ion_row + radius * quad[rot[0]]
    points = points - jnp.round(points)
    gathered[me, :, pl.ds(0, columns)] = inv[...]
    gathered[me, :, pl.ds(columns, LANES)] = jnp.zeros((1, LANES), jnp.float32)
    for part, value in enumerate(in_three(points)):
        for d in range(3):
            first = columns + (part * 3 + d) * quad_count
            gathered[me, :, first : first + quad_count] = value[d : d + 1, :]

    pl.semaphore_wait(barrier, count - 1)

    def copy_a(slot, i):
        return pltpu.make_async_remote_copy(
            src_ref=gathered.at[me], dst_ref=gathered.at[slot],
            send_sem=send_a.at[i], recv_sem=recv_a.at[slot],
            device_id=peer(i)[1], device_id_type=MESH,
        )

    def send_rows(i, carry):
        copy_a(me, i).start()
        return carry

    lax.fori_loop(1, count, send_rows, 0)

    waves[...] = jnp.zeros_like(waves)
    waves[0:3, :] = triples[...].astype(jnp.float32)
    row = lax.broadcasted_iota(jnp.int32, (LANES, 16), 0)
    column = lax.broadcasted_iota(jnp.int32, (LANES, 16), 1)
    component = lax.rem(row // quad_count, 3)
    choose = jnp.where((component == column) & (row < 9 * quad_count), 1.0, 0.0)
    choose = choose.astype(jnp.bfloat16)
    for c in range(chunks):
        part = waves[:, c * span : (c + 1) * span].astype(jnp.bfloat16)
        spread[c] = jnp.dot(choose, part, preferred_element_type=jnp.float32).astype(jnp.bfloat16)
    acc[...] = jnp.zeros_like(acc)

    def receive_rows(i, carry):
        source = peer(i)[0]
        copy_a(source, i).wait_recv()
        return carry

    lax.fori_loop(1, count, receive_rows, 0)

    everything = gathered[...].reshape(count, columns + LANES)
    for part, value in enumerate(in_three(everything[:, :columns])):
        rows[part * count : (part + 1) * count, :] = value.astype(jnp.bfloat16)
    parts = everything[:, columns:]
    place = lax.rem(lax.broadcasted_iota(jnp.int32, parts.shape, 1), quad_count)
    for k in range(quad_count):
        mine = jnp.where(place == k, parts, 0.0).astype(jnp.bfloat16)
        phase_lhs[k * count : (k + 1) * count, :] = mine

    def one_chunk(c, carry):
        coef_copy(c).wait()
        for i in range(2):
            product = lax.dot_general(rows[...], held[c, i], LAST, preferred_element_type=jnp.float32)
            weight[i] = (product[:count] + product[count : 2 * count]) + product[2 * count :]
        angle[...] = jnp.dot(phase_lhs[...], spread[c], preferred_element_type=jnp.float32)
        for e in range(0, count, 8):
            w0 = weight[0, e : e + 8, :]
            w1 = weight[1, e : e + 8, :]
            acc[quad_count, e : e + 8, :] += fold(w0)
            for k in range(quad_count):
                turns = angle[k * count + e : k * count + e + 8, :]
                r = turns - jnp.round(turns)
                z = r * r
                sine = r * (SIN[0] + z * (SIN[1] + z * SIN[2]))
                cosine = COS[0] + z * (COS[1] + z * (COS[2] + z * COS[3]))
                acc[k, e : e + 8, :] += fold(sine * (w1 * cosine - w0 * sine))
        return carry

    lax.fori_loop(0, chunks, one_chunk, 0)

    place = lax.broadcasted_iota(jnp.int32, (count, LANES), 1)
    share = jnp.sum(acc[quad_count], axis=1, keepdims=True)
    share = jnp.broadcast_to(share, (count, LANES))
    for k in range(quad_count):
        share = share + jnp.where(place == k, jnp.sum(acc[k], axis=1, keepdims=True), 0.0)
    total[...] = share

    def copy_b(target, slot, i, device):
        return pltpu.make_async_remote_copy(
            src_ref=outgoing.at[target], dst_ref=incoming.at[slot],
            send_sem=send_b.at[i], recv_sem=recv_b.at[slot],
            device_id=device, device_id_type=MESH,
        )

    def send_share(i, carry):
        target, device = peer(i)
        outgoing[target] = total[pl.ds(target, 1), :]
        copy_b(target, me, i, device).start()
        return carry

    lax.fori_loop(1, count, send_share, 0)
    incoming[me] = total[pl.ds(me, 1), :]

    def receive_share(i, carry):
        source, device = peer(i)
        copy_b(source, source, i, device).wait_recv()
        return carry

    lax.fori_loop(1, count, receive_share, 0)
    out[...] = jnp.sum(incoming[...], axis=0)[:, :quad_count]

    def drain(i, carry):
        target, device = peer(i)
        copy_a(me, i).wait_send()
        copy_b(target, me, i, device).wait_send()
        return carry

    lax.fori_loop(1, count, drain, 0)


def fold(x):
    tiles = [x[:, j : j + LANES] for j in range(0, x.shape[1], LANES)]
    while len(tiles) > 1:
        pairs = [a + b for a, b in zip(tiles[0::2], tiles[1::2])]
        tiles = pairs + tiles[len(pairs) * 2 :]
    return tiles[0]


def on_device(mesh_shape, coef, triples, elec, ions, assign, rot, quad, inv):
    n_ga, n_orb = mesh_shape
    count = n_ga * n_orb
    quad_count = quad.shape[2]
    local, columns = coef.shape[1:]
    assert inv.shape[0] == 1 and 9 * quad_count <= LANES
    span = math.gcd(local, 1024)
    chunks = local // span
    smem = pl.BlockSpec(memory_space=pltpu.SMEM)
    vmem = pl.BlockSpec(memory_space=pltpu.VMEM)
    dma = pltpu.SemaphoreType.DMA
    return pl.pallas_call(
        functools.partial(kernel, n_ga, n_orb, quad_count),
        out_shape=jax.ShapeDtypeStruct((1, quad_count), jnp.float32),
        in_specs=[pl.BlockSpec(memory_space=pl.ANY), vmem, vmem, vmem, smem, smem, vmem, vmem],
        out_specs=vmem,
        scratch_shapes=[
            pltpu.VMEM((chunks, 2, span, columns), jnp.bfloat16),
            dma((chunks,)),
            pltpu.VMEM((count, 1, columns + LANES), jnp.float32),
            pltpu.VMEM((16, local), jnp.float32),
            pltpu.VMEM((chunks, LANES, span), jnp.bfloat16),
            pltpu.VMEM((3 * count, columns), jnp.bfloat16),
            pltpu.VMEM((quad_count * count, LANES), jnp.bfloat16),
            pltpu.VMEM((2, count, span), jnp.float32),
            pltpu.VMEM((quad_count * count, span), jnp.float32),
            pltpu.VMEM((quad_count + 1, count, LANES), jnp.float32),
            pltpu.VMEM((count, LANES), jnp.float32),
            pltpu.VMEM((count, 1, LANES), jnp.float32),
            pltpu.VMEM((count, 1, LANES), jnp.float32),
            dma((count,)),
            dma((count,)),
            dma((count,)),
            dma((count,)),
        ],
        compiler_params=pltpu.CompilerParams(
            collective_id=0, has_side_effects=True, vmem_limit_bytes=50 * 1024 * 1024
        ),
        name="ratios",
    )(coef, triples, elec, ions, assign, rot, quad, inv)


def solution(mesh):
    sizes = (mesh.shape["ga"], mesh.shape["orb"])
    return jax.shard_map(
        functools.partial(on_device, sizes),
        mesh=mesh,
        in_specs=(
            P(None, ("ga", "orb"), None),
            P(None, ("ga", "orb")),
            P(None, ("ga", "orb")),
            P(),
            P(("ga", "orb")),
            P(("ga", "orb")),
            P(),
            P(("ga", "orb"), None),
        ),
        out_specs=P(("ga", "orb"), None),
        check_vma=False,
    )
```

```python
import functools
import math

import jax
import jax.numpy as jnp
from jax import lax
from jax.experimental import pallas as pl
from jax.experimental.pallas import tpu as pltpu
from jax.sharding import PartitionSpec as P

MESH = pl.DeviceIdType.MESH
LANES = 128
SIN = (4.4409175764498094, -7.256811405668293, 3.2296557608294836)
COS = (1.4141797907346831, -6.976861782062955, 5.7090010941235345, -1.7141125404832036)
LAST = (((1,), (1,)), ((), ()))


ROUNDER = 1.5 * 2.0**23


def in_three(x):
    high = x.astype(jnp.bfloat16).astype(jnp.float32)
    rest = x - high
    middle = rest.astype(jnp.bfloat16).astype(jnp.float32)
    return high, middle, (rest - middle).astype(jnp.bfloat16).astype(jnp.float32)


def rounded(x):
    return (x + ROUNDER) - ROUNDER


def each_peer(count, step):
    if count <= 32:
        for i in range(1, count):
            step(i)
    else:

        def body(i, carry):
            step(i)
            return carry

        lax.fori_loop(1, count, body, 0)


def kernel(
    n_ga, n_orb, quad_count,
    coef, triples_in, elec_in, ions_in, assign, rot, quad_in, inv_in, out,
    held, held_sem, triples, elec, ions, quad, inv, small_sem,
    gathered, waves, spread, rows, phase_lhs, weight_a, angle_a, weight_b, angle_b, acc,
    outgoing, incoming, send_a, recv_a, send_b, recv_b,
):
    count = n_ga * n_orb
    me = lax.axis_index("ga") * n_orb + lax.axis_index("orb")
    chunks, _, span, columns = held.shape

    def coef_copy(c):
        return pltpu.make_async_copy(
            coef.at[:, pl.ds(c * span, span), :], held.at[c], held_sem.at[c]
        )

    def peer(i):
        other = lax.rem(me + i, count)
        return other, (other // n_orb, lax.rem(other, n_orb))

    small = [
        pltpu.make_async_copy(src, dst, small_sem.at[i])
        for i, (src, dst) in enumerate(
            [(ions_in, ions), (elec_in, elec), (quad_in, quad), (inv_in, inv), (triples_in, triples)]
        )
    ]
    for copy in small:
        copy.start()
    barrier = pltpu.get_barrier_semaphore()

    def greet(i):
        pl.semaphore_signal(barrier, inc=1, device_id=peer(i)[1], device_id_type=MESH)

    each_peer(count, greet)
    for c in range(chunks):
        coef_copy(c).start()
    for copy in small:
        copy.wait()

    lane = lax.broadcasted_iota(jnp.int32, ions.shape, 1)
    ion = jnp.sum(jnp.where(lane == assign[0], ions[...], 0.0), axis=1, keepdims=True)
    square = None
    for d in range(3):
        offset = elec[0:1, d : d + 1] - ion[d : d + 1, :]
        square = offset * offset if square is None else square + offset * offset
    radius = jnp.sqrt(square)
    lane = lax.broadcasted_iota(jnp.int32, (quad_count, LANES), 1)
    within = lax.rem(lane, 3 * quad_count)
    k_of = lax.broadcasted_iota(jnp.int32, (quad_count, LANES), 0)
    chosen = lax.broadcasted_iota(jnp.int32, quad.shape[1:], 1) == rot[0]
    points = jnp.zeros((quad_count, LANES), jnp.float32)
    for d in range(3):
        move = jnp.sum(jnp.where(chosen, quad[d], 0.0), axis=1, keepdims=True)
        located = ion[d : d + 1, :] + radius * move
        points = points + jnp.where(within == d * quad_count + k_of, located, 0.0)
    points = jnp.sum(points, axis=0, keepdims=True)
    high, middle, low = in_three(points - rounded(points))
    lane = lax.broadcasted_iota(jnp.int32, (1, LANES), 1)
    size = 3 * quad_count
    parts = jnp.where(lane < size, high, jnp.where(lane < 2 * size, middle, low))
    gathered[me, :, pl.ds(0, columns)] = inv[...]
    gathered[me, :, pl.ds(columns, LANES)] = jnp.where(lane < 3 * size, parts, 0.0)

    waves[...] = jnp.zeros_like(waves)
    waves[0:3, :] = triples[...].astype(jnp.float32)
    row = lax.broadcasted_iota(jnp.int32, (LANES, 16), 0)
    column = lax.broadcasted_iota(jnp.int32, (LANES, 16), 1)
    component = lax.rem(row // quad_count, 3)
    choose = jnp.where((component == column) & (row < 9 * quad_count), 1.0, 0.0)
    choose = choose.astype(jnp.bfloat16)
    for c in range(chunks):
        part = waves[:, c * span : (c + 1) * span].astype(jnp.bfloat16)
        spread[c] = jnp.dot(choose, part, preferred_element_type=jnp.float32).astype(jnp.bfloat16)
    acc[...] = jnp.zeros_like(acc)

    pl.semaphore_wait(barrier, count - 1)

    def send_row(i):
        pltpu.make_async_remote_copy(
            src_ref=gathered.at[me], dst_ref=gathered.at[me],
            send_sem=send_a, recv_sem=recv_a,
            device_id=peer(i)[1], device_id_type=MESH,
        ).start()

    each_peer(count, send_row)

    def wait_others(buffer, sem):
        others = buffer.at[pl.ds(0, count - 1)]
        pltpu.make_async_copy(others, others, sem).wait()

    wait_others(gathered, recv_a)

    everything = gathered[...].reshape(count, columns + LANES)
    for part, value in enumerate(in_three(everything[:, :columns])[:2]):
        rows[part * count : (part + 1) * count, :] = value.astype(jnp.bfloat16)
    parts = everything[:, columns:]
    place = lax.rem(lax.broadcasted_iota(jnp.int32, parts.shape, 1), quad_count)
    for k in range(quad_count):
        mine = jnp.where(place == k, parts, 0.0).astype(jnp.bfloat16)
        phase_lhs[k * count : (k + 1) * count, :] = mine

    width = math.gcd(span, 256)
    pieces = span // width
    tiles = count // 8

    def produce(c, weight, angle, piece):
        cols = slice(piece * width, (piece + 1) * width)
        for i in range(2):
            product = lax.dot_general(
                rows[...], held[c, i, cols, :], LAST, preferred_element_type=jnp.float32
            )
            weight[i, :, cols] = product[:count] + product[count:]
        angle[:, cols] = jnp.dot(
            phase_lhs[...], spread[c, :, cols], preferred_element_type=jnp.float32
        )

    def consume(weight, angle, tile):
        e = tile * 8
        w0 = weight[0, e : e + 8, :]
        w1 = weight[1, e : e + 8, :]
        acc[quad_count, e : e + 8, :] += fold(w0)
        for k in range(quad_count):
            turns = angle[k * count + e : k * count + e + 8, :]
            r = turns - rounded(turns)
            z = r * r
            sine = r * (SIN[0] + z * (SIN[1] + z * SIN[2]))
            cosine = COS[0] + z * (COS[1] + z * (COS[2] + z * COS[3]))
            acc[k, e : e + 8, :] += fold(sine * (w1 * cosine - w0 * sine))

    def both(now, c, later):
        coef_copy(c).wait()
        for tile in range(tiles):
            for piece in range(tile * pieces // tiles, (tile + 1) * pieces // tiles):
                produce(c, *later, piece)
            consume(*now, tile)

    even, odd = (weight_a, angle_a), (weight_b, angle_b)
    coef_copy(0).wait()
    for piece in range(pieces):
        produce(0, *even, piece)

    def two_chunks(i, carry):
        both(even, 2 * i + 1, odd)
        both(odd, 2 * i + 2, even)
        return carry

    lax.fori_loop(0, (chunks - 1) // 2, two_chunks, 0)
    last = even
    if chunks % 2 == 0:
        both(even, chunks - 1, odd)
        last = odd
    for tile in range(tiles):
        consume(*last, tile)

    place = lax.broadcasted_iota(jnp.int32, (count, LANES), 1)
    share = jnp.sum(acc[quad_count], axis=1, keepdims=True)
    share = jnp.broadcast_to(share, (count, LANES))
    for k in range(quad_count):
        share = share + jnp.where(place == k, jnp.sum(acc[k], axis=1, keepdims=True), 0.0)
    outgoing[...] = share.reshape(count, 1, LANES)

    def send_share(i):
        target, device = peer(i)
        pltpu.make_async_remote_copy(
            src_ref=outgoing.at[target], dst_ref=incoming.at[me],
            send_sem=send_b, recv_sem=recv_b,
            device_id=device, device_id_type=MESH,
        ).start()

    each_peer(count, send_share)
    incoming[me] = outgoing[me]
    wait_others(gathered, send_a)
    wait_others(incoming, recv_b)
    out[...] = jnp.sum(incoming[...], axis=0)[:, :quad_count]
    wait_others(outgoing, send_b)


def fold(x):
    tiles = [x[:, j : j + LANES] for j in range(0, x.shape[1], LANES)]
    while len(tiles) > 1:
        pairs = [a + b for a, b in zip(tiles[0::2], tiles[1::2])]
        tiles = pairs + tiles[len(pairs) * 2 :]
    return tiles[0]


def on_device(mesh_shape, coef, triples, elec, ions, assign, rot, quad, inv):
    n_ga, n_orb = mesh_shape
    count = n_ga * n_orb
    quad_count = quad.shape[2]
    local, columns = coef.shape[1:]
    assert inv.shape[0] == 1 and 9 * quad_count <= LANES
    span = math.gcd(local, 1024)
    chunks = local // span
    smem = pl.BlockSpec(memory_space=pltpu.SMEM)
    hbm = pl.BlockSpec(memory_space=pltpu.HBM)
    dma = pltpu.SemaphoreType.DMA
    elec = elec.T
    quad = jnp.transpose(quad, (1, 2, 0))
    weight = pltpu.VMEM((2, count, span), jnp.float32)
    angle = pltpu.VMEM((quad_count * count, span), jnp.float32)
    return pl.pallas_call(
        functools.partial(kernel, n_ga, n_orb, quad_count),
        out_shape=jax.ShapeDtypeStruct((1, quad_count), jnp.float32),
        in_specs=[hbm, hbm, hbm, hbm, smem, smem, hbm, hbm],
        out_specs=pl.BlockSpec(memory_space=pltpu.VMEM),
        scratch_shapes=[
            pltpu.VMEM((chunks, 2, span, columns), jnp.bfloat16),
            dma((chunks,)),
            pltpu.VMEM(triples.shape, jnp.int32),
            pltpu.VMEM(elec.shape, jnp.float32),
            pltpu.VMEM(ions.shape, jnp.float32),
            pltpu.VMEM(quad.shape, jnp.float32),
            pltpu.VMEM(inv.shape, jnp.float32),
            dma((5,)),
            pltpu.VMEM((count, 1, columns + LANES), jnp.float32),
            pltpu.VMEM((16, local), jnp.float32),
            pltpu.VMEM((chunks, LANES, span), jnp.bfloat16),
            pltpu.VMEM((2 * count, columns), jnp.bfloat16),
            pltpu.VMEM((quad_count * count, LANES), jnp.bfloat16),
            weight,
            angle,
            weight,
            angle,
            pltpu.VMEM((quad_count + 1, count, LANES), jnp.float32),
            pltpu.VMEM((count, 1, LANES), jnp.float32),
            pltpu.VMEM((count, 1, LANES), jnp.float32),
            dma,
            dma,
            dma,
            dma,
        ],
        compiler_params=pltpu.CompilerParams(
            collective_id=0, has_side_effects=True, vmem_limit_bytes=60 * 1024 * 1024
        ),
        name="ratios",
    )(coef, triples, elec, ions, assign, rot, quad, inv)


def solution(mesh):
    sizes = (mesh.shape["ga"], mesh.shape["orb"])
    return jax.shard_map(
        functools.partial(on_device, sizes),
        mesh=mesh,
        in_specs=(
            P(None, ("ga", "orb"), None),
            P(None, ("ga", "orb")),
            P(None, ("ga", "orb")),
            P(),
            P(("ga", "orb")),
            P(("ga", "orb")),
            P(),
            P(("ga", "orb"), None),
        ),
        out_specs=P(("ga", "orb"), None),
        check_vma=False,
    )
```

```python
import functools
import math

import jax
import jax.numpy as jnp
from jax import lax
from jax.experimental import pallas as pl
from jax.experimental.pallas import tpu as pltpu
from jax.sharding import PartitionSpec as P

MESH = pl.DeviceIdType.MESH
LANES = 128
SIN = (4.4409175764498094, -7.256811405668293, 3.2296557608294836)
COS = (1.4141797907346831, -6.976861782062955, 5.7090010941235345, -1.7141125404832036)
LAST = (((1,), (1,)), ((), ()))


ROUNDER = 1.5 * 2.0**23


def in_three(x):
    high = x.astype(jnp.bfloat16).astype(jnp.float32)
    rest = x - high
    middle = rest.astype(jnp.bfloat16).astype(jnp.float32)
    return high, middle, (rest - middle).astype(jnp.bfloat16).astype(jnp.float32)


def rounded(x):
    return (x + ROUNDER) - ROUNDER


def each_peer(count, step):
    if count <= 32:
        for i in range(1, count):
            step(i)
    else:

        def body(i, carry):
            step(i)
            return carry

        lax.fori_loop(1, count, body, 0)


def kernel(
    n_ga, n_orb, quad_count,
    coef, triples_in, elec_in, ions_in, assign, rot, quad_in, inv_in, out,
    held, held_sem, triples, elec, ions, quad, inv, small_sem,
    gathered, waves, spread, rows, phase_lhs, weight_a, angle_a, weight_b, angle_b, acc,
    outgoing, incoming, send_a, recv_a, send_b, recv_b,
):
    count = n_ga * n_orb
    me = lax.axis_index("ga") * n_orb + lax.axis_index("orb")
    chunks, _, span, columns = held.shape

    def coef_copy(c):
        return pltpu.make_async_copy(
            coef.at[:, pl.ds(c * span, span), :], held.at[c], held_sem.at[c]
        )

    def peer(i):
        other = lax.rem(me + i, count)
        return other, (other // n_orb, lax.rem(other, n_orb))

    small = [
        pltpu.make_async_copy(src, dst, small_sem.at[i])
        for i, (src, dst) in enumerate(
            [(ions_in, ions), (elec_in, elec), (quad_in, quad), (inv_in, inv), (triples_in, triples)]
        )
    ]
    for copy in small:
        copy.start()
    barrier = pltpu.get_barrier_semaphore()

    def greet(i):
        pl.semaphore_signal(barrier, inc=1, device_id=peer(i)[1], device_id_type=MESH)

    each_peer(count, greet)
    for c in range(chunks):
        coef_copy(c).start()
    for copy in small[:-1]:
        copy.wait()

    lane = lax.broadcasted_iota(jnp.int32, ions.shape, 1)
    ion = jnp.sum(jnp.where(lane == assign[0], ions[...], 0.0), axis=1, keepdims=True)
    square = None
    for d in range(3):
        offset = elec[0:1, d : d + 1] - ion[d : d + 1, :]
        square = offset * offset if square is None else square + offset * offset
    radius = jnp.sqrt(square)
    lane = lax.broadcasted_iota(jnp.int32, (quad_count, LANES), 1)
    within = lax.rem(lane, 3 * quad_count)
    k_of = lax.broadcasted_iota(jnp.int32, (quad_count, LANES), 0)
    chosen = lax.broadcasted_iota(jnp.int32, quad.shape[1:], 1) == rot[0]
    points = jnp.zeros((quad_count, LANES), jnp.float32)
    for d in range(3):
        move = jnp.sum(jnp.where(chosen, quad[d], 0.0), axis=1, keepdims=True)
        located = ion[d : d + 1, :] + radius * move
        points = points + jnp.where(within == d * quad_count + k_of, located, 0.0)
    points = jnp.sum(points, axis=0, keepdims=True)
    high, middle, low = in_three(points - rounded(points))
    lane = lax.broadcasted_iota(jnp.int32, (1, LANES), 1)
    size = 3 * quad_count
    parts = jnp.where(lane < size, high, jnp.where(lane < 2 * size, middle, low))
    gathered[me, :, pl.ds(0, columns)] = inv[...]
    gathered[me, :, pl.ds(columns, LANES)] = jnp.where(lane < 3 * size, parts, 0.0)

    pl.semaphore_wait(barrier, count - 1)

    def send_row(i):
        pltpu.make_async_remote_copy(
            src_ref=gathered.at[me], dst_ref=gathered.at[me],
            send_sem=send_a, recv_sem=recv_a,
            device_id=peer(i)[1], device_id_type=MESH,
        ).start()

    each_peer(count, send_row)

    small[-1].wait()
    waves[...] = jnp.zeros_like(waves)
    waves[0:3, :] = triples[...].astype(jnp.float32)
    row = lax.broadcasted_iota(jnp.int32, (LANES, 16), 0)
    column = lax.broadcasted_iota(jnp.int32, (LANES, 16), 1)
    component = lax.rem(row // quad_count, 3)
    choose = jnp.where((component == column) & (row < 9 * quad_count), 1.0, 0.0)
    choose = choose.astype(jnp.bfloat16)
    for c in range(chunks):
        part = waves[:, c * span : (c + 1) * span].astype(jnp.bfloat16)
        spread[c] = jnp.dot(choose, part, preferred_element_type=jnp.float32).astype(jnp.bfloat16)
    acc[...] = jnp.zeros_like(acc)

    def wait_others(buffer, sem):
        others = buffer.at[pl.ds(0, count - 1)]
        pltpu.make_async_copy(others, others, sem).wait()

    wait_others(gathered, recv_a)

    everything = gathered[...].reshape(count, columns + LANES)
    for part, value in enumerate(in_three(everything[:, :columns])[:2]):
        rows[part * count : (part + 1) * count, :] = value.astype(jnp.bfloat16)
    parts = everything[:, columns:]
    place = lax.rem(lax.broadcasted_iota(jnp.int32, parts.shape, 1), quad_count)
    for k in range(quad_count):
        mine = jnp.where(place == k, parts, 0.0).astype(jnp.bfloat16)
        phase_lhs[k * count : (k + 1) * count, :] = mine

    width = math.gcd(span, 256)
    pieces = span // width
    tiles = count // 8

    def produce(c, weight, angle, piece):
        cols = slice(piece * width, (piece + 1) * width)
        for i in range(2):
            product = lax.dot_general(
                rows[...], held[c, i, cols, :], LAST, preferred_element_type=jnp.float32
            )
            weight[i, :, cols] = product[:count] + product[count:]
        angle[:, cols] = jnp.dot(
            phase_lhs[...], spread[c, :, cols], preferred_element_type=jnp.float32
        )

    def consume(weight, angle, tile):
        e = tile * 8
        w0 = weight[0, e : e + 8, :]
        w1 = weight[1, e : e + 8, :]
        acc[quad_count, e : e + 8, :] += fold(w0)
        for k in range(quad_count):
            turns = angle[k * count + e : k * count + e + 8, :]
            r = turns - rounded(turns)
            z = r * r
            sine = r * (SIN[0] + z * (SIN[1] + z * SIN[2]))
            cosine = COS[0] + z * (COS[1] + z * (COS[2] + z * COS[3]))
            acc[k, e : e + 8, :] += fold(sine * (w1 * cosine - w0 * sine))

    def both(now, c, later):
        coef_copy(c).wait()
        for tile in range(tiles):
            for piece in range(tile * pieces // tiles, (tile + 1) * pieces // tiles):
                produce(c, *later, piece)
            consume(*now, tile)

    even, odd = (weight_a, angle_a), (weight_b, angle_b)
    coef_copy(0).wait()
    for piece in range(pieces):
        produce(0, *even, piece)

    def two_chunks(i, carry):
        both(even, 2 * i + 1, odd)
        both(odd, 2 * i + 2, even)
        return carry

    lax.fori_loop(0, (chunks - 1) // 2, two_chunks, 0)
    last = even
    if chunks % 2 == 0:
        both(even, chunks - 1, odd)
        last = odd
    for tile in range(tiles):
        consume(*last, tile)

    place = lax.broadcasted_iota(jnp.int32, (count, LANES), 1)
    share = jnp.sum(acc[quad_count], axis=1, keepdims=True)
    share = jnp.broadcast_to(share, (count, LANES))
    for k in range(quad_count):
        share = share + jnp.where(place == k, jnp.sum(acc[k], axis=1, keepdims=True), 0.0)
    outgoing[...] = share.reshape(count, 1, LANES)

    def send_share(i):
        target, device = peer(i)
        pltpu.make_async_remote_copy(
            src_ref=outgoing.at[target], dst_ref=incoming.at[me],
            send_sem=send_b, recv_sem=recv_b,
            device_id=device, device_id_type=MESH,
        ).start()

    each_peer(count, send_share)
    incoming[me] = outgoing[me]
    wait_others(gathered, send_a)
    wait_others(incoming, recv_b)
    out[...] = jnp.sum(incoming[...], axis=0)[:, :quad_count]
    wait_others(outgoing, send_b)


def fold(x):
    tiles = [x[:, j : j + LANES] for j in range(0, x.shape[1], LANES)]
    while len(tiles) > 1:
        pairs = [a + b for a, b in zip(tiles[0::2], tiles[1::2])]
        tiles = pairs + tiles[len(pairs) * 2 :]
    return tiles[0]


def on_device(mesh_shape, coef, triples, elec, ions, assign, rot, quad, inv):
    n_ga, n_orb = mesh_shape
    count = n_ga * n_orb
    quad_count = quad.shape[2]
    local, columns = coef.shape[1:]
    assert inv.shape[0] == 1 and 9 * quad_count <= LANES
    span = math.gcd(local, 1024)
    chunks = local // span
    smem = pl.BlockSpec(memory_space=pltpu.SMEM)
    hbm = pl.BlockSpec(memory_space=pltpu.HBM)
    dma = pltpu.SemaphoreType.DMA
    elec = elec.T
    quad = jnp.transpose(quad, (1, 2, 0))
    weight = pltpu.VMEM((2, count, span), jnp.float32)
    angle = pltpu.VMEM((quad_count * count, span), jnp.float32)
    return pl.pallas_call(
        functools.partial(kernel, n_ga, n_orb, quad_count),
        out_shape=pltpu.VMEM((1, quad_count), jnp.float32),
        in_specs=[hbm, hbm, hbm, hbm, smem, smem, hbm, hbm],
        out_specs=pl.BlockSpec(memory_space=pltpu.VMEM),
        scratch_shapes=[
            pltpu.VMEM((chunks, 2, span, columns), jnp.bfloat16),
            dma((chunks,)),
            pltpu.VMEM(triples.shape, jnp.int32),
            pltpu.VMEM(elec.shape, jnp.float32),
            pltpu.VMEM(ions.shape, jnp.float32),
            pltpu.VMEM(quad.shape, jnp.float32),
            pltpu.VMEM(inv.shape, jnp.float32),
            dma((5,)),
            pltpu.VMEM((count, 1, columns + LANES), jnp.float32),
            pltpu.VMEM((16, local), jnp.float32),
            pltpu.VMEM((chunks, LANES, span), jnp.bfloat16),
            pltpu.VMEM((2 * count, columns), jnp.bfloat16),
            pltpu.VMEM((quad_count * count, LANES), jnp.bfloat16),
            weight,
            angle,
            weight,
            angle,
            pltpu.VMEM((quad_count + 1, count, LANES), jnp.float32),
            pltpu.VMEM((count, 1, LANES), jnp.float32),
            pltpu.VMEM((count, 1, LANES), jnp.float32),
            dma,
            dma,
            dma,
            dma,
        ],
        compiler_params=pltpu.CompilerParams(
            collective_id=0, has_side_effects=True, vmem_limit_bytes=60 * 1024 * 1024
        ),
        name="ratios",
    )(coef, triples, elec, ions, assign, rot, quad, inv)


def solution(mesh):
    sizes = (mesh.shape["ga"], mesh.shape["orb"])
    return jax.shard_map(
        functools.partial(on_device, sizes),
        mesh=mesh,
        in_specs=(
            P(None, ("ga", "orb"), None),
            P(None, ("ga", "orb")),
            P(None, ("ga", "orb")),
            P(),
            P(("ga", "orb")),
            P(("ga", "orb")),
            P(),
            P(("ga", "orb"), None),
        ),
        out_specs=P(("ga", "orb"), None),
        check_vma=False,
    )
```

```python
import functools
import math

import jax
import jax.numpy as jnp
from jax import lax
from jax.experimental import pallas as pl
from jax.experimental.pallas import tpu as pltpu
from jax.sharding import PartitionSpec as P

MESH = pl.DeviceIdType.MESH
LANES = 128
SIN = (6.281280240499966, -41.09525634382307, 73.58572901915015)
ATAN = (
    0.15913366845101437, -0.052569633937468316, 0.02867321820152353,
    -0.01355301556095631, 0.003317582793410697,
)
LAST = (((1,), (1,)), ((), ()))


ROUNDER = 1.5 * 2.0**23


def in_three(x):
    high = x.astype(jnp.bfloat16).astype(jnp.float32)
    rest = x - high
    middle = rest.astype(jnp.bfloat16).astype(jnp.float32)
    return high, middle, (rest - middle).astype(jnp.bfloat16).astype(jnp.float32)


def rounded(x):
    return (x + ROUNDER) - ROUNDER


def polar(x, y):
    across, along = jnp.abs(y), jnp.abs(x)
    largest = jnp.maximum(across, along)
    q = jnp.minimum(across, along) / jnp.maximum(largest, 1e-37)
    z = q * q
    turns = ATAN[4]
    for term in ATAN[3::-1]:
        turns = term + z * turns
    turns = q * turns
    turns = jnp.where(across > along, 0.25 - turns, turns)
    turns = jnp.where(x < 0, 0.5 - turns, turns)
    return largest * jnp.sqrt(1.0 + z), jnp.where(y < 0, -turns, turns)


def each_peer(count, step):
    if count <= 32:
        for i in range(1, count):
            step(i)
    else:

        def body(i, carry):
            step(i)
            return carry

        lax.fori_loop(1, count, body, 0)


def kernel(
    n_ga, n_orb, quad_count,
    coef, triples_in, elec_in, ions_in, assign, rot, quad_in, inv_in, out,
    held, held_sem, triples, elec, ions, quad, inv, small_sem,
    gathered, waves, spread, rows, phase_lhs, weight_a, angle_a, weight_b, angle_b, acc,
    outgoing, incoming, send_a, recv_a, send_b, recv_b,
):
    count = n_ga * n_orb
    me = lax.axis_index("ga") * n_orb + lax.axis_index("orb")
    chunks, _, span, columns = held.shape

    def coef_copy(c):
        return pltpu.make_async_copy(
            coef.at[:, pl.ds(c * span, span), :], held.at[c], held_sem.at[c]
        )

    def peer(i):
        other = lax.rem(me + i, count)
        return other, (other // n_orb, lax.rem(other, n_orb))

    small = [
        pltpu.make_async_copy(src, dst, small_sem.at[i])
        for i, (src, dst) in enumerate(
            [(ions_in, ions), (elec_in, elec), (quad_in, quad), (inv_in, inv), (triples_in, triples)]
        )
    ]
    for copy in small:
        copy.start()
    barrier = pltpu.get_barrier_semaphore()

    def greet(i):
        pl.semaphore_signal(barrier, inc=1, device_id=peer(i)[1], device_id_type=MESH)

    each_peer(count, greet)
    for c in range(chunks):
        coef_copy(c).start()
    for copy in small[:-1]:
        copy.wait()

    lane = lax.broadcasted_iota(jnp.int32, ions.shape, 1)
    ion = jnp.sum(jnp.where(lane == assign[0], ions[...], 0.0), axis=1, keepdims=True)
    square = None
    for d in range(3):
        offset = elec[0:1, d : d + 1] - ion[d : d + 1, :]
        square = offset * offset if square is None else square + offset * offset
    radius = jnp.sqrt(square)
    lane = lax.broadcasted_iota(jnp.int32, (quad_count, LANES), 1)
    within = lax.rem(lane, 3 * quad_count)
    k_of = lax.broadcasted_iota(jnp.int32, (quad_count, LANES), 0)
    chosen = lax.broadcasted_iota(jnp.int32, quad.shape[1:], 1) == rot[0]
    points = jnp.zeros((quad_count, LANES), jnp.float32)
    for d in range(3):
        move = jnp.sum(jnp.where(chosen, quad[d], 0.0), axis=1, keepdims=True)
        located = ion[d : d + 1, :] + radius * move
        points = points + jnp.where(within == d * quad_count + k_of, located, 0.0)
    points = jnp.sum(points, axis=0, keepdims=True)
    high, middle, low = in_three(points - rounded(points))
    lane = lax.broadcasted_iota(jnp.int32, (1, LANES), 1)
    size = 3 * quad_count
    parts = jnp.where(lane < size, high, jnp.where(lane < 2 * size, middle, low))
    gathered[me, :, pl.ds(0, columns)] = inv[...]
    gathered[me, :, pl.ds(columns, LANES)] = jnp.where(lane < 3 * size, parts, 0.0)

    pl.semaphore_wait(barrier, count - 1)

    def send_row(i):
        pltpu.make_async_remote_copy(
            src_ref=gathered.at[me], dst_ref=gathered.at[me],
            send_sem=send_a, recv_sem=recv_a,
            device_id=peer(i)[1], device_id_type=MESH,
        ).start()

    each_peer(count, send_row)

    small[-1].wait()
    waves[...] = jnp.zeros_like(waves)
    waves[0:3, :] = triples[...].astype(jnp.float32)
    row = lax.broadcasted_iota(jnp.int32, (LANES, 16), 0)
    column = lax.broadcasted_iota(jnp.int32, (LANES, 16), 1)
    component = lax.rem(row // quad_count, 3)
    choose = jnp.where((component == column) & (row < 9 * quad_count), 1.0, 0.0)
    choose = choose.astype(jnp.bfloat16)
    for c in range(chunks):
        part = waves[:, c * span : (c + 1) * span].astype(jnp.bfloat16)
        spread[c] = jnp.dot(choose, part, preferred_element_type=jnp.float32).astype(jnp.bfloat16)
    acc[...] = jnp.zeros_like(acc)

    def wait_others(buffer, sem):
        others = buffer.at[pl.ds(0, count - 1)]
        pltpu.make_async_copy(others, others, sem).wait()

    wait_others(gathered, recv_a)

    everything = gathered[...].reshape(count, columns + LANES)
    for part, value in enumerate(in_three(everything[:, :columns])[:2]):
        rows[part * count : (part + 1) * count, :] = value.astype(jnp.bfloat16)
    parts = everything[:, columns:]
    place = lax.rem(lax.broadcasted_iota(jnp.int32, parts.shape, 1), quad_count)
    for k in range(quad_count):
        mine = jnp.where(place == k, parts, 0.0).astype(jnp.bfloat16)
        phase_lhs[k * count : (k + 1) * count, :] = mine

    width = math.gcd(span, 256)
    pieces = span // width
    tiles = count // 8

    def produce(c, weight, angle, piece):
        cols = slice(piece * width, (piece + 1) * width)
        w = []
        for i in range(2):
            product = lax.dot_general(
                rows[...], held[c, i, cols, :], LAST, preferred_element_type=jnp.float32
            )
            w.append(product[:count] + product[count:])
        weight[0, :, cols], weight[1, :, cols] = polar(*w)
        angle[:, cols] = jnp.dot(
            phase_lhs[...], spread[c, :, cols], preferred_element_type=jnp.float32
        )

    def consume(weight, angle, tile):
        e = tile * 8
        size = weight[0, e : e + 8, :]
        shift = weight[1, e : e + 8, :]
        for k in range(quad_count):
            turns = angle[k * count + e : k * count + e + 8, :] - shift
            v = 0.25 - jnp.abs(turns - rounded(turns))
            z = v * v
            acc[k, e : e + 8, :] += fold((size * v) * (SIN[0] + z * (SIN[1] + z * SIN[2])))

    def both(now, c, later):
        coef_copy(c).wait()
        for tile in range(tiles):
            for piece in range(tile * pieces // tiles, (tile + 1) * pieces // tiles):
                produce(c, *later, piece)
            consume(*now, tile)

    even, odd = (weight_a, angle_a), (weight_b, angle_b)
    coef_copy(0).wait()
    for piece in range(pieces):
        produce(0, *even, piece)

    def two_chunks(i, carry):
        both(even, 2 * i + 1, odd)
        both(odd, 2 * i + 2, even)
        return carry

    lax.fori_loop(0, (chunks - 1) // 2, two_chunks, 0)
    last = even
    if chunks % 2 == 0:
        both(even, chunks - 1, odd)
        last = odd
    for tile in range(tiles):
        consume(*last, tile)

    place = lax.broadcasted_iota(jnp.int32, (count, LANES), 1)
    share = jnp.zeros((count, LANES), jnp.float32)
    for k in range(quad_count):
        share = share + jnp.where(place == k, jnp.sum(acc[k], axis=1, keepdims=True), 0.0)
    outgoing[...] = share.reshape(count, 1, LANES)

    def send_share(i):
        target, device = peer(i)
        pltpu.make_async_remote_copy(
            src_ref=outgoing.at[target], dst_ref=incoming.at[me],
            send_sem=send_b, recv_sem=recv_b,
            device_id=device, device_id_type=MESH,
        ).start()

    each_peer(count, send_share)
    incoming[me] = outgoing[me]
    wait_others(gathered, send_a)
    wait_others(incoming, recv_b)
    out[...] = jnp.sum(incoming[...], axis=0)[:, :quad_count]
    wait_others(outgoing, send_b)


def fold(x):
    tiles = [x[:, j : j + LANES] for j in range(0, x.shape[1], LANES)]
    while len(tiles) > 1:
        pairs = [a + b for a, b in zip(tiles[0::2], tiles[1::2])]
        tiles = pairs + tiles[len(pairs) * 2 :]
    return tiles[0]


def on_device(mesh_shape, coef, triples, elec, ions, assign, rot, quad, inv):
    n_ga, n_orb = mesh_shape
    count = n_ga * n_orb
    quad_count = quad.shape[2]
    local, columns = coef.shape[1:]
    assert inv.shape[0] == 1 and 9 * quad_count <= LANES
    span = math.gcd(local, 1024)
    chunks = local // span
    smem = pl.BlockSpec(memory_space=pltpu.SMEM)
    hbm = pl.BlockSpec(memory_space=pltpu.HBM)
    dma = pltpu.SemaphoreType.DMA
    elec = elec.T
    quad = jnp.transpose(quad, (1, 2, 0))
    weight = pltpu.VMEM((2, count, span), jnp.float32)
    angle = pltpu.VMEM((quad_count * count, span), jnp.float32)
    return pl.pallas_call(
        functools.partial(kernel, n_ga, n_orb, quad_count),
        out_shape=pltpu.VMEM((1, quad_count), jnp.float32),
        in_specs=[hbm, hbm, hbm, hbm, smem, smem, hbm, hbm],
        out_specs=pl.BlockSpec(memory_space=pltpu.VMEM),
        scratch_shapes=[
            pltpu.VMEM((chunks, 2, span, columns), jnp.bfloat16),
            dma((chunks,)),
            pltpu.VMEM(triples.shape, jnp.int32),
            pltpu.VMEM(elec.shape, jnp.float32),
            pltpu.VMEM(ions.shape, jnp.float32),
            pltpu.VMEM(quad.shape, jnp.float32),
            pltpu.VMEM(inv.shape, jnp.float32),
            dma((5,)),
            pltpu.VMEM((count, 1, columns + LANES), jnp.float32),
            pltpu.VMEM((16, local), jnp.float32),
            pltpu.VMEM((chunks, LANES, span), jnp.bfloat16),
            pltpu.VMEM((2 * count, columns), jnp.bfloat16),
            pltpu.VMEM((quad_count * count, LANES), jnp.bfloat16),
            weight,
            angle,
            weight,
            angle,
            pltpu.VMEM((quad_count, count, LANES), jnp.float32),
            pltpu.VMEM((count, 1, LANES), jnp.float32),
            pltpu.VMEM((count, 1, LANES), jnp.float32),
            dma,
            dma,
            dma,
            dma,
        ],
        compiler_params=pltpu.CompilerParams(
            collective_id=0, has_side_effects=True, vmem_limit_bytes=60 * 1024 * 1024
        ),
        name="ratios",
    )(coef, triples, elec, ions, assign, rot, quad, inv)


def solution(mesh):
    sizes = (mesh.shape["ga"], mesh.shape["orb"])
    return jax.shard_map(
        functools.partial(on_device, sizes),
        mesh=mesh,
        in_specs=(
            P(None, ("ga", "orb"), None),
            P(None, ("ga", "orb")),
            P(None, ("ga", "orb")),
            P(),
            P(("ga", "orb")),
            P(("ga", "orb")),
            P(),
            P(("ga", "orb"), None),
        ),
        out_specs=P(("ga", "orb"), None),
        check_vma=False,
    )
```
